256 devices in a mesh: ctx: 32 (over z, x), head: 8 (over y, core).
Axes of the slice: x: 4, y: 4, z: 8, core: 2. Of those that a mesh axis runs over, the one named last changes fastest.
Arguments:
- queries: bfloat16 [98304, 1024], P('ctx', 'head'), may hold values from -6 to 6
- keys: bfloat16 [98304, 1024], P('ctx', 'head'), may hold values from -6 to 6
- values: bfloat16 [98304, 1024], P('ctx', 'head'), may hold values from -6 to 6
- prefix: int32 [1], replicated, may hold values from 24576 to 73727
- norm_gain: float32 [1024], P('head'), may hold values from 0.1 to 1.9
- out_weight: bfloat16 [1024, 4096], P(None, 'head'), may hold values from -0.1875 to 0.1875
Outputs:
- projected: bfloat16 [98304, 4096], P('ctx', 'head')
The draws below stay inside these ranges and needn't reach their ends.
All inputs are finite; a program needn't handle non-finite values.
Results may differ from the reference program's by a relative error of at most 0.0049.
Values may be sent and summed in bfloat16 or wider, within the bound.
A program may use at most 64 MiB of HBM per device.

```python
import jax
import jax.numpy as jnp
from jax import lax

D = 4096
HD = 128
GROUP = 512
H = 8
SEQ = 98304


def shard_levels(stream_key, shape, cuts, low, largest):
    loudness = 1.0
    for axis_at, blocks in cuts:
        steps = jax.random.uniform(jax.random.fold_in(jax.random.fold_in(stream_key, 6), axis_at), (blocks,), jnp.float32, low / len(cuts), largest / len(cuts))
        loudness = loudness * jnp.repeat(jnp.exp(steps), shape[axis_at] // blocks).reshape((-1,) + (1,) * (len(shape) - 1 - axis_at))
    return loudness


def gaussian(rng, dims, scale, most, split=(), kind=jnp.bfloat16):
    values = jax.random.normal(rng, dims, jnp.float32) * scale
    if len(split) > 0:
        values = shard_levels(rng, dims, split, -0.22, 0.18) * values
    return jnp.clip(values, min=-most, max=most).astype(kind)


def setup_inputs(seed: int = 0) -> dict:
    splits = jax.random.split(jax.random.key(seed), 7)
    return {
        "queries": gaussian(splits[0], (SEQ, H * HD), 1.0, 6.0, ((0, 32), (1, 8))),
        "keys": gaussian(splits[1], (SEQ, H * HD), 1.0, 6.0, ((0, 32), (1, 8))),
        "values": gaussian(splits[2], (SEQ, H * HD), 1.0, 6.0, ((0, 32), (1, 8))),
        "prefix": jax.random.randint(splits[3], (1,), SEQ // 4, 3 * SEQ // 4).astype(jnp.int32),
        "norm_gain": jnp.clip(1.0 + 0.18 * jax.random.normal(splits[4], (H * HD,), jnp.float32), 0.1, 1.9),
        "out_weight": gaussian(splits[5], (H * HD, D), (H * HD) ** -0.5, 0.1875, ((1, 8),)),
    }


def reference(queries, keys, values, prefix, norm_gain, out_weight):
    seq_length = queries.shape[0]
    blocks = seq_length // GROUP
    query_blocks = queries.reshape(blocks, GROUP, H, HD)
    key_blocks = keys.reshape(blocks, GROUP, H, HD)
    value_blocks = values.reshape(blocks, GROUP, H, HD)
    positions = jnp.arange(seq_length, dtype=jnp.int32).reshape(blocks, GROUP)
    inside = positions < prefix[0]
    lower_mask = jnp.tril(jnp.ones((GROUP, GROUP), dtype=bool))

    def prefix_step(running, block_inputs):
        key_block, value_block, inside_block = block_inputs
        masked_keys = key_block * inside_block[:, None, None].astype(jnp.bfloat16)
        return (running + jnp.einsum('chd,che->hde', masked_keys.astype(jnp.float32), value_block.astype(jnp.float32), precision=lax.Precision.HIGHEST), None)
    prefix_state, _ = lax.scan(prefix_step, jnp.zeros((H, HD, HD), jnp.float32), (key_blocks, value_blocks, inside))

    def block_step(carried, block_inputs):
        query_block, key_block, value_block, inside_block = block_inputs
        query_as_float = query_block.astype(jnp.float32)
        key_as_float = key_block.astype(jnp.float32)
        value_float = value_block.astype(jnp.float32)
        preceding_tokens = jnp.einsum('chd,hde->che', query_as_float, carried, precision=lax.Precision.HIGHEST)
        attention_scores = jnp.einsum('ujr,ejr->jue', query_as_float, key_as_float, precision=lax.Precision.HIGHEST)
        weights = jnp.where(lower_mask[None], attention_scores, 0.0).astype(jnp.bfloat16)
        local_part = jnp.einsum('hcm,mhe->che', weights.astype(jnp.float32), value_float, precision=lax.Precision.HIGHEST)
        prefix_read = jnp.einsum('chd,hde->che', query_as_float, prefix_state, precision=lax.Precision.HIGHEST)
        attended = jnp.where(inside_block[:, None, None], prefix_read, preceding_tokens + local_part)
        updated = carried + jnp.einsum('chd,che->hde', key_as_float, value_float, precision=lax.Precision.HIGHEST)
        return (updated, attended)
    _, attended = lax.scan(block_step, jnp.zeros((H, HD, HD), jnp.float32), (query_blocks, key_blocks, value_blocks, inside))
    mean_square = lax.optimization_barrier(jnp.mean(attended * attended, axis=-1, keepdims=True))
    head_normalized = attended * lax.rsqrt(mean_square + 1e-06) * norm_gain.reshape(H, HD)
    head_normalized = head_normalized.astype(jnp.bfloat16).reshape(seq_length, H * HD)
    return jnp.dot(head_normalized, out_weight, preferred_element_type=jnp.float32).astype(jnp.bfloat16)
```

```python
import jax
import jax.numpy as jnp
from jax import lax
from jax.experimental import pallas as pl
from jax.experimental.pallas import tpu as pltpu
from jax.sharding import PartitionSpec as P

MESH = pl.DeviceIdType.MESH
HD = 128
X, Y, Z, CORES = 4, 4, 8, 2
HEADS = Y * CORES
ROWS = 3072
COLS = 512
SUB = 256
SUBS = ROWS // SUB
PART = 512
PARTS = ROWS // PART
HALF = PART // 2
AHEAD = 2
QUARTER = HD // X
NT = (((1,), (1,)), ((), ()))
TN = (((0,), (0,)), ((), ()))
F32, BF16 = jnp.float32, jnp.bfloat16

FROM_LEFT, FROM_RIGHT, FAR_A, FAR_B, SIB_OWN, SIB_LEFT, SIB_RIGHT, SIB_A, SIB_B = range(9)


def split_two(x):
    high = x.astype(BF16)
    return jnp.concatenate([high, (x - high.astype(F32)).astype(BF16)], axis=1)


def dot_two(rows, halves):
    both = jnp.dot(rows, halves, preferred_element_type=F32)
    return both[:, :HD] + both[:, HD:]


def kernel(
    q_hbm, k_hbm, v_hbm, prefix_ref, gain_ref, w_hbm, out_hbm,
    q, k, v, w, out, local, gathered, total, earlier, own_masked, read_state,
    got1, sums, got2, give3, got3,
    load_sem, out_sem, ex_send, ex_recv, ring_send, ring_recv,
):
    ctx, head = lax.axis_index("ctx"), lax.axis_index("head")
    z, x = ctx // X, ctx % X
    y, core = head // CORES, head % CORES

    x_peers = [(z * X + (x + s) % X, head) for s in range(1, X)]
    z_peers = [(((z + s) % Z) * X + x, head) for s in range(1, Z)]
    right = (ctx, ((y + 1) % Y) * CORES + core)
    left = (ctx, ((y + Y - 1) % Y) * CORES + core)
    sibling = (ctx, y * CORES + 1 - core)

    barrier = pltpu.get_barrier_semaphore()
    everyone = x_peers + z_peers + [right, left, sibling]
    for peer in everyone:
        pl.semaphore_signal(barrier, inc=1, device_id=peer, device_id_type=MESH)

    loads = [
        pltpu.make_async_copy(src, dst, load_sem.at[i])
        for i, (src, dst) in enumerate([(k_hbm, k), (v_hbm, v), (q_hbm, q), (w_hbm, w)])
    ]
    for load in loads:
        load.start()

    prefix = prefix_ref[0]
    base = ctx * ROWS

    def inside(block):
        at = base + block * SUB + lax.broadcasted_iota(jnp.int32, (SUB, HD), 0)
        return at < prefix

    loads[0].wait()
    loads[1].wait()

    def state(block, carry):
        rows = pl.ds(block * SUB, SUB)
        vals = v[rows, :]
        masked = jnp.where(inside(block), vals, jnp.zeros_like(vals))
        earlier[block] = split_two(carry[:, :HD])
        return carry + lax.dot_general(
            k[rows, :], jnp.concatenate([vals, masked], axis=1), TN, preferred_element_type=F32
        )

    summed = lax.fori_loop(0, SUBS, state, jnp.zeros((HD, 2 * HD), F32))
    total[...] = summed
    own_masked[...] = split_two(summed[:, HD:])
    mine = pl.ds(pl.multiple_of(x * QUARTER, QUARTER), QUARTER)
    got1[x] = total[mine, :]

    pl.semaphore_wait(barrier, len(everyone))

    def exchange(src, dst, slot, peer):
        return pltpu.make_async_remote_copy(
            src_ref=src, dst_ref=dst, send_sem=ex_send.at[slot], recv_sem=ex_recv.at[slot],
            device_id=peer, device_id_type=MESH,
        )

    first = []
    for s in range(1, X):
        quarter = pl.ds(pl.multiple_of(((x + s) % X) * QUARTER, QUARTER), QUARTER)
        first.append(exchange(total.at[quarter], got1.at[x], s - 1, x_peers[s - 1]))
        first[-1].start()

    loads[2].wait()
    row_at = lax.broadcasted_iota(jnp.int32, (SUB, SUB), 0)
    col_at = lax.broadcasted_iota(jnp.int32, (SUB, SUB), 1)

    def causal(block, _):
        rows = pl.ds(block * SUB, SUB)
        queries = q[rows, :]
        scores = lax.dot_general(queries, k[rows, :], NT, preferred_element_type=F32)
        weights = jnp.where(col_at <= row_at, scores, 0.0).astype(BF16)
        near = jnp.dot(weights, v[rows, :], preferred_element_type=F32)
        near = near + dot_two(queries, earlier[block])
        local[rows, :] = jnp.where(inside(block), dot_two(queries, own_masked[...]), near)
        return 0

    lax.fori_loop(0, 4, causal, 0)

    for moved in first:
        moved.wait_recv()
    along_x = got1[0] + got1[1] + got1[2] + got1[3]
    sums[0] = along_x[:, :HD]
    sums[1] = along_x[:, HD:]

    second = []
    for s in range(1, Z):
        second.append(exchange(sums.at[(z + s) // Z], got2.at[s - 1], X - 2 + s, z_peers[s - 1]))
        second[-1].start()

    lax.fori_loop(4, 9, causal, 0)

    for moved in second:
        moved.wait_recv()
    along_z = got2[0]
    for s in range(1, Z - 1):
        along_z = along_z + got2[s]
    for to in range(X):
        part = along_z
        for s in range(X):
            if s < to:
                part = part + got1[s][:, :HD]
            elif s > to:
                part = part + got1[s][:, HD:]
        give3[to] = part
    got3[x] = give3[x]

    third = []
    for s in range(1, X):
        third.append(exchange(give3.at[(x + s) % X], got3.at[x], X + Z - 3 + s, x_peers[s - 1]))
        third[-1].start()

    lax.fori_loop(9, SUBS, causal, 0)

    for moved in third:
        moved.wait_recv()
    read_state[...] = split_two(got3[...].reshape(HD, HD))
    loads[3].wait()

    left_head = ((y + Y - 1) % Y) * CORES + core
    right_head = ((y + 1) % Y) * CORES + core
    far_head = ((y + 2) % Y) * CORES + core

    def copy(block, slot):
        heads, first_row, count, peer = (
            (head, 0, PART, right),
            (head, 0, PART, left),
            (left_head, 0, HALF, right),
            (right_head, HALF, HALF, left),
            (head, 0, PART, sibling),
            (left_head, 0, PART, sibling),
            (right_head, 0, PART, sibling),
            (far_head, 0, HALF, sibling),
            (far_head, HALF, HALF, sibling),
        )[slot]
        piece = gathered.at[heads, pl.ds(pl.multiple_of(block * PART + first_row, HALF), count)]
        return pltpu.make_async_remote_copy(
            src_ref=piece, dst_ref=piece,
            send_sem=ring_send.at[block, slot], recv_sem=ring_recv.at[block, slot],
            device_id=peer, device_id_type=MESH,
        )

    gain = gain_ref[...]

    def norm(block):
        rows = pl.ds(pl.multiple_of(block * PART, PART), PART)
        attended = dot_two(q[rows, :], read_state[...]) + local[rows, :]
        mean_square = jnp.mean(attended * attended, axis=-1, keepdims=True)
        normed = attended * lax.rsqrt(mean_square + 1e-06) * gain
        gathered[head, rows, :] = normed.astype(BF16)
        for slot in (FROM_LEFT, FROM_RIGHT, SIB_OWN):
            copy(block, slot).start()

    def forward(block):
        copy(block, FROM_LEFT).wait_recv()
        copy(block, FAR_A).start()
        copy(block, SIB_LEFT).start()
        copy(block, FROM_RIGHT).wait_recv()
        copy(block, FAR_B).start()
        copy(block, SIB_RIGHT).start()

    def pass_far(block):
        copy(block, FAR_A).wait_recv()
        copy(block, SIB_A).start()
        copy(block, FAR_B).wait_recv()
        copy(block, SIB_B).start()

    def store(block):
        rows = pl.ds(pl.multiple_of(block * PART, PART), PART)
        return pltpu.make_async_copy(out.at[rows], out_hbm.at[rows], out_sem.at[block])

    def project(block):
        for slot in (SIB_OWN, SIB_LEFT, SIB_RIGHT, SIB_A, SIB_B):
            copy(block, slot).wait_recv()
        rows = pl.ds(pl.multiple_of(block * PART, PART), PART)
        normed = jnp.concatenate([gathered[h, rows, :] for h in range(HEADS)], axis=1)
        out[rows, :] = jnp.dot(normed, w[...], preferred_element_type=F32).astype(BF16)
        store(block).start()

    def step(t, _):
        @pl.when(t < PARTS)
        def _():
            norm(t)

        @pl.when((t >= AHEAD) & (t < PARTS + AHEAD))
        def _():
            forward(t - AHEAD)

        @pl.when((t >= AHEAD + 2) & (t < PARTS + AHEAD + 2))
        def _():
            project(t - AHEAD - 2)

        @pl.when((t >= AHEAD + 1) & (t < PARTS + AHEAD + 1))
        def _():
            pass_far(t - AHEAD - 1)

        return 0

    lax.fori_loop(0, PARTS + AHEAD + 2, step, 0)

    for moved in first + second + third:
        moved.wait_send()

    def drain(block, _):
        for slot in range(9):
            copy(block, slot).wait_send()
        store(block).wait()
        return 0

    lax.fori_loop(0, PARTS, drain, 0)


def body(queries, keys, values, prefix, norm_gain, out_weight):
    hbm = pl.BlockSpec(memory_space=pl.ANY)
    exchanges = 2 * (X - 1) + Z - 1
    return pl.pallas_call(
        kernel,
        out_shape=jax.ShapeDtypeStruct((ROWS, COLS), BF16),
        in_specs=[
            hbm, hbm, hbm,
            pl.BlockSpec(memory_space=pltpu.SMEM),
            pl.BlockSpec(memory_space=pltpu.VMEM),
            hbm,
        ],
        out_specs=hbm,
        scratch_shapes=[
            pltpu.VMEM((ROWS, HD), BF16),
            pltpu.VMEM((ROWS, HD), BF16),
            pltpu.VMEM((ROWS, HD), BF16),
            pltpu.VMEM((HEADS * HD, COLS), BF16),
            pltpu.VMEM((ROWS, COLS), BF16),
            pltpu.VMEM((ROWS, HD), F32),
            pltpu.VMEM((HEADS, ROWS, HD), BF16),
            pltpu.VMEM((HD, 2 * HD), F32),
            pltpu.VMEM((SUBS, HD, 2 * HD), BF16),
            pltpu.VMEM((HD, 2 * HD), BF16),
            pltpu.VMEM((HD, 2 * HD), BF16),
            pltpu.VMEM((X, QUARTER, 2 * HD), F32),
            pltpu.VMEM((2, QUARTER, HD), F32),
            pltpu.VMEM((Z - 1, QUARTER, HD), F32),
            pltpu.VMEM((X, QUARTER, HD), F32),
            pltpu.VMEM((X, QUARTER, HD), F32),
            pltpu.SemaphoreType.DMA((4,)),
            pltpu.SemaphoreType.DMA((PARTS,)),
            pltpu.SemaphoreType.DMA((exchanges,)),
            pltpu.SemaphoreType.DMA((exchanges,)),
            pltpu.SemaphoreType.DMA((PARTS, 9)),
            pltpu.SemaphoreType.DMA((PARTS, 9)),
        ],
        compiler_params=pltpu.CompilerParams(
            collective_id=0, has_side_effects=True, vmem_limit_bytes=40 * 2**20
        ),
        cost_estimate=pl.CostEstimate(
            flops=2 * ROWS * (8 * HD * COLS + 1024 * HD), bytes_accessed=8 * 2**20, transcendentals=ROWS
        ),
    )(queries, keys, values, prefix, norm_gain.reshape(1, HD), out_weight)


def solution(mesh):
    return jax.shard_map(
        body,
        mesh=mesh,
        in_specs=(
            P("ctx", "head"),
            P("ctx", "head"),
            P("ctx", "head"),
            P(),
            P("head"),
            P(None, "head"),
        ),
        out_specs=P("ctx", "head"),
        check_vma=False,
    )
```

```python
import jax
import jax.numpy as jnp
from jax import lax
from jax.experimental import pallas as pl
from jax.experimental.pallas import tpu as pltpu
from jax.sharding import PartitionSpec as P

MESH = pl.DeviceIdType.MESH
HD = 128
X, Y, Z, CORES = 4, 4, 8, 2
HEADS = Y * CORES
ROWS = 3072
COLS = 512
SUB = 256
SUBS = ROWS // SUB
LATE = (512, 512, 512, 512)
EARLY = ROWS - sum(LATE)
EARLY_HALF = EARLY // 2
LATE_FROM = tuple(EARLY + sum(LATE[:i]) for i in range(len(LATE)))
STATE_ROWS = HD + 16
LOCAL_AT, STATE_AT, NORMED_AT = EARLY, 2 * EARLY, 2 * EARLY + STATE_ROWS
SHIFT = NORMED_AT - EARLY
GATHERED = ROWS + SHIFT
PARTS = [
    (0, EARLY_HALF),
    (EARLY_HALF, EARLY_HALF),
    (LOCAL_AT, EARLY_HALF),
    (LOCAL_AT + EARLY_HALF, EARLY_HALF),
    (STATE_AT, STATE_ROWS),
] + [(SHIFT + start, count) for start, count in zip(LATE_FROM, LATE)]
STATE, FIRST_LATE = 4, 5
DIRECT = (STATE,)
BESIDE_FIRST = 4
AHEAD_GIVEN, LATER_GIVEN = 3, 1
AHEAD_Z = 3
STEP = EARLY // 4
QUARTER = HD // X
NT = (((1,), (1,)), ((), ()))
TN = (((0,), (0,)), ((), ()))
F32, BF16 = jnp.float32, jnp.bfloat16

FROM_LEFT, FROM_RIGHT, FAR_A, FAR_B, SIB_OWN, SIB_LEFT, SIB_RIGHT, SIB_A, SIB_B = range(9)


def split_two(x):
    high = x.astype(BF16)
    return jnp.concatenate([high, (x - high.astype(F32)).astype(BF16)], axis=1)


def dot_two(rows, halves):
    both = jnp.dot(rows, halves, preferred_element_type=F32)
    return both[:, :HD] + both[:, HD:]


def normalize(attended, gain):
    mean_square = jnp.mean(attended * attended, axis=-1, keepdims=True)
    return (attended * lax.rsqrt(mean_square + 1e-06) * gain).astype(BF16)


def kernel(
    q_hbm, k_hbm, v_hbm, prefix_ref, gain_hbm, w_hbm, out,
    q, k, v, w, gain_ref, local, gathered, total, earlier, own_masked, read_state,
    got1, sums, got2, give3, got3,
    near_sem, far_sem, load_sem, ex_send, ex_recv, ring_send, ring_recv,
):
    ctx, head = lax.axis_index("ctx"), lax.axis_index("head")
    z, x = ctx // X, ctx % X
    y, core = head // CORES, head % CORES

    x_peers = [(z * X + (x + s) % X, head) for s in range(1, X)]
    z_peers = [(((z + s) % Z) * X + x, head) for s in range(1, Z)]
    up, down = (y + 1) % Y, (y + Y - 1) % Y
    right, left = (ctx, up * CORES + core), (ctx, down * CORES + core)
    far = (ctx, ((y + 2) % Y) * CORES + core)
    sibling = (ctx, y * CORES + 1 - core)

    barrier = pltpu.get_barrier_semaphore()
    for s in range(1, Y):
        pl.semaphore_signal(
            barrier, inc=1, device_id=(ctx, ((y + s) % Y) * CORES), device_id_type=MESH
        )

    @pl.when(core == 1)
    def _():
        pl.semaphore_signal(barrier, inc=1, device_id=sibling, device_id_type=MESH)

    for peer in x_peers:
        pl.semaphore_signal(barrier, inc=1, device_id=peer, device_id_type=MESH)
    for peer, _ in z_peers:
        pl.semaphore_signal(barrier, inc=1, device_id=(peer, y * CORES + 1), device_id_type=MESH)

    loads = [
        pltpu.make_async_copy(src, dst, load_sem.at[i])
        for i, (src, dst) in enumerate([
            (q_hbm.at[pl.ds(0, EARLY)], gathered.at[head, pl.ds(0, EARLY)]),
            (q_hbm, q), (gain_hbm, gain_ref), (w_hbm, w),
        ] + [
            (src.at[pl.ds(i * ROWS // 2, ROWS // 2)], dst.at[pl.ds(i * ROWS // 2, ROWS // 2)])
            for i in range(2) for src, dst in ((k_hbm, k), (v_hbm, v))
        ])
    ]
    early_load, q_load, gain_load, w_load = loads[:4]
    ahead = z < AHEAD_Z
    for load in loads[4:]:
        load.start()

    far_head = ((y + 2) % Y) * CORES + core
    left_head, right_head = down * CORES + core, up * CORES + core

    def copy(part, slot):
        start, count = PARTS[part]
        direct = part in DIRECT
        upper = count if direct else (count // 2 + 15) // 16 * 16
        heads, first, count, peer = (
            (head, start, count, right),
            (head, start, count, left),
            (head, start, count, far) if direct else (left_head, start, upper, right),
            (right_head, start + upper, count - upper, left),
            (head, start, count, sibling),
            (left_head, start, count, sibling),
            (right_head, start, count, sibling),
            (far_head, start, upper, sibling),
            (far_head, start + upper, count - upper, sibling),
        )[slot]
        piece = gathered.at[heads, pl.ds(first, count)]
        return pltpu.make_async_remote_copy(
            src_ref=piece, dst_ref=piece,
            send_sem=ring_send.at[part, slot], recv_sem=ring_recv.at[part, slot],
            device_id=peer, device_id_type=MESH,
        )

    def slots(part):
        return [slot for slot in range(9) if part not in DIRECT or slot not in (FAR_B, SIB_B)]

    def give(part):
        if part in DIRECT:
            copy(part, FAR_A).start()
        for slot in (FROM_LEFT, FROM_RIGHT, SIB_OWN):
            copy(part, slot).start()

    def forward(part):
        copy(part, FROM_LEFT).wait_recv()
        if part not in DIRECT:
            copy(part, FAR_A).start()
        copy(part, SIB_LEFT).start()
        copy(part, FROM_RIGHT).wait_recv()
        if part not in DIRECT:
            copy(part, FAR_B).start()
        copy(part, SIB_RIGHT).start()

    def pass_far(part):
        copy(part, FAR_A).wait_recv()
        copy(part, SIB_A).start()
        if part not in DIRECT:
            copy(part, FAR_B).wait_recv()
            copy(part, SIB_B).start()

    def arrived(*parts):
        for part in parts:
            for slot in slots(part):
                if slot >= SIB_OWN:
                    copy(part, slot).wait_recv()

    def meet():
        @pl.when(core == 0)
        def _():
            pl.semaphore_signal(near_sem, inc=1, device_id=sibling, device_id_type=MESH)

        @pl.when(core == 1)
        def _():
            pl.semaphore_wait(near_sem, 1)

    prefix = prefix_ref[0]
    base = ctx * ROWS

    def inside(block):
        at = base + block * SUB + lax.broadcasted_iota(jnp.int32, (SUB, HD), 0)
        return at < prefix

    def state(block, carry):
        rows = pl.ds(block * SUB, SUB)
        vals = v[rows, :]
        masked = jnp.where(inside(block), vals, jnp.zeros_like(vals))
        earlier[block] = split_two(carry[:, :HD])
        return carry + lax.dot_general(
            k[rows, :], jnp.concatenate([vals, masked], axis=1), TN, preferred_element_type=F32
        )

    loads[4].wait()
    loads[5].wait()
    pl.when(ahead)(early_load.start)
    q_load.start()
    gain_load.start()
    w_load.start()
    summed = lax.fori_loop(0, SUBS // 2, state, jnp.zeros((HD, 2 * HD), F32))
    loads[6].wait()
    loads[7].wait()
    summed = lax.fori_loop(SUBS // 2, SUBS, state, summed)
    total[...] = summed
    own_masked[...] = split_two(summed[:, HD:])
    mine = pl.ds(pl.multiple_of(x * QUARTER, QUARTER), QUARTER)
    got1[x] = total[mine, :]

    row_at = lax.broadcasted_iota(jnp.int32, (SUB, SUB), 0)
    col_at = lax.broadcasted_iota(jnp.int32, (SUB, SUB), 1)

    def causal(block, _):
        rows = pl.ds(block * SUB, SUB)
        queries = q[rows, :]
        scores = lax.dot_general(queries, k[rows, :], NT, preferred_element_type=F32)
        weights = jnp.where(col_at <= row_at, scores, 0.0).astype(BF16)
        near = jnp.dot(weights, v[rows, :], preferred_element_type=F32)
        near = near + dot_two(queries, earlier[block])
        local[rows, :] = jnp.where(inside(block), dot_two(queries, own_masked[...]), near)
        return 0

    def give_local():
        for half in range(2):
            rows = slice(half * EARLY_HALF, (half + 1) * EARLY_HALF)
            at = LOCAL_AT + half * EARLY_HALF
            gathered[head, at:at + EARLY_HALF, :] = local[rows, :].astype(BF16)
            give(2 + half)

    @pl.when(core == 0)
    def _():
        pl.semaphore_wait(barrier, 1 + (Y - 1) * CORES + X - 1)

    @pl.when(ahead)
    def _():
        meet()
        early_load.wait()
        give(0)
        give(1)
        q_load.wait()
        lax.fori_loop(0, EARLY // SUB, causal, 0)
        give_local()


    @pl.when(core == 1)
    def _():
        pl.semaphore_wait(barrier, CORES * (Z - 1) + X - 1)

    def exchange(src, dst, slot, peer):
        return pltpu.make_async_remote_copy(
            src_ref=src, dst_ref=dst, send_sem=ex_send.at[slot], recv_sem=ex_recv.at[slot],
            device_id=peer, device_id_type=MESH,
        )

    first = []
    for s in range(1, X):
        quarter = pl.ds(pl.multiple_of(((x + s) % X) * QUARTER, QUARTER), QUARTER)
        first.append(exchange(total.at[quarter], got1.at[x], s - 1, x_peers[s - 1]))
        first[-1].start()

    @pl.when(~ahead)
    def _():
        meet()

    @pl.when(core == 1)
    def _():
        pl.semaphore_signal(far_sem, inc=1, device_id=sibling, device_id_type=MESH)

    @pl.when(~ahead)
    def _():
        q_load.wait()
        lax.fori_loop(0, BESIDE_FIRST, causal, 0)

    @pl.when(ahead)
    def _():
        forward(0)

    for moved in first:
        moved.wait_recv()
    along_x = got1[0] + got1[1] + got1[2] + got1[3]
    sums[0] = along_x[:, :HD].astype(BF16)
    sums[1] = along_x[:, HD:].astype(BF16)

    @pl.when(core == 0)
    def _():
        pl.semaphore_wait(far_sem, 1)

    second = []
    for s in range(1, Z):
        second.append(exchange(sums.at[(z + s) // Z], got2.at[s - 1], X - 2 + s, z_peers[s - 1]))
        second[-1].start()

    @pl.when(ahead)
    def _():
        lax.fori_loop(EARLY // SUB, SUBS, causal, 0)
        forward(1)

    @pl.when(~ahead)
    def _():
        lax.fori_loop(BESIDE_FIRST, SUBS, causal, 0)

    for moved in second:
        moved.wait_recv()
    along_z = got2[0].astype(F32)
    for s in range(1, Z - 1):
        along_z = along_z + got2[s].astype(F32)
    for to in range(X):
        part = along_z
        for s in range(X):
            if s < to:
                part = part + got1[s][:, :HD]
            elif s > to:
                part = part + got1[s][:, HD:]
        give3[to] = part
    got3[x] = give3[x]

    third = []
    for s in range(1, X):
        third.append(exchange(give3.at[(x + s) % X], got3.at[x], X + Z - 3 + s, x_peers[s - 1]))
        third[-1].start()

    @pl.when(ahead)
    def _():
        forward(2)
        forward(3)

    for moved in third:
        moved.wait_recv()
    read_state[...] = split_two(got3[...].reshape(HD, HD))

    gain_load.wait()
    gain = gain_ref[...]

    def give_state():
        gathered[head, STATE_AT:STATE_AT + HD, :] = read_state[:, :HD]
        gain_high = gain.astype(BF16).astype(F32)
        gain_row = lax.broadcasted_iota(jnp.int32, (16, HD), 0)
        gathered[head, STATE_AT + HD:NORMED_AT, :] = jnp.where(
            gain_row == 0, gain_high, jnp.where(gain_row == 1, gain - gain_high, 0.0)
        ).astype(BF16)
        give(STATE)

    def rows_of(part):
        start, count = PARTS[part]
        start = start - SHIFT if part >= FIRST_LATE else start
        return slice(start, start + count)

    def place_of(part):
        start, count = PARTS[part]
        return slice(start, start + count)

    def norm(part):
        rows = rows_of(part)
        attended = dot_two(q[rows, :], read_state[...]) + local[rows, :]
        gathered[head, place_of(part), :] = normalize(attended, gain)
        give(part)

    def project(part):
        normed = jnp.concatenate([gathered[h, place_of(part), :] for h in range(HEADS)], axis=1)
        out[rows_of(part), :] = jnp.dot(normed, w[...], preferred_element_type=F32).astype(BF16)

    def early(step, _):
        rows = pl.ds(pl.multiple_of(step * STEP, 16), STEP)
        local_rows = pl.ds(pl.multiple_of(LOCAL_AT + step * STEP, 16), STEP)
        normed = []
        for h in range(HEADS):
            gains = gathered[h, STATE_AT + HD:NORMED_AT, :].astype(F32)
            attended = jnp.dot(
                gathered[h, rows, :], gathered[h, STATE_AT:STATE_AT + HD, :], preferred_element_type=F32
            ) + gathered[h, local_rows, :].astype(F32)
            normed.append(normalize(attended, gains[0:1] + gains[1:2]))
        out[rows, :] = jnp.dot(
            jnp.concatenate(normed, axis=1), w[...], preferred_element_type=F32
        ).astype(BF16)
        return 0

    w_load.wait()
    late = list(range(FIRST_LATE, len(PARTS)))

    def drain(parts):
        for part in parts:
            for slot in slots(part):
                copy(part, slot).wait_send()

    def stream(parts, given, between):
        for i, part in enumerate(parts):
            if i + given < len(parts):
                norm(parts[i + given])
            forward(part)
            between(i)
            if i > 1:
                arrived(parts[i - 2])
                project(parts[i - 2])
            if i > 0:
                pass_far(parts[i - 1])
        arrived(parts[-2])
        project(parts[-2])
        pass_far(parts[-1])
        arrived(parts[-1])
        project(parts[-1])

    @pl.when(ahead)
    def _():
        give_state()
        for part in late[:AHEAD_GIVEN]:
            norm(part)
        for part in range(4):
            pass_far(part)
        forward(STATE)
        pass_far(STATE)
        arrived(0, 2, STATE)
        lax.fori_loop(0, 2, early, 0)

        def between(i):
            if i == 0:
                arrived(1, 3)
                lax.fori_loop(2, 4, early, 0)

        stream(late, AHEAD_GIVEN, between)
        drain(range(len(PARTS)))

    @pl.when(~ahead)
    def _():
        parts = [0, 1] + late
        for part in parts[:LATER_GIVEN]:
            norm(part)
        stream(parts, LATER_GIVEN, lambda i: None)
        drain(parts)

    for moved in first + second + third:
        moved.wait_send()


def body(queries, keys, values, prefix, norm_gain, out_weight):
    def hbm(array):
        return pltpu.with_memory_space_constraint(array, pltpu.HBM)

    anywhere = pl.BlockSpec(memory_space=pl.ANY)
    exchanges = 2 * (X - 1) + Z - 1
    return pl.pallas_call(
        kernel,
        out_shape=pltpu.VMEM((ROWS, COLS), BF16),
        in_specs=[
            anywhere, anywhere, anywhere,
            pl.BlockSpec(memory_space=pltpu.SMEM),
            anywhere, anywhere,
        ],
        out_specs=pl.BlockSpec(memory_space=pltpu.VMEM),
        scratch_shapes=[
            pltpu.VMEM((ROWS, HD), BF16),
            pltpu.VMEM((ROWS, HD), BF16),
            pltpu.VMEM((ROWS, HD), BF16),
            pltpu.VMEM((HEADS * HD, COLS), BF16),
            pltpu.VMEM((1, HD), F32),
            pltpu.VMEM((ROWS, HD), F32),
            pltpu.VMEM((HEADS, GATHERED, HD), BF16),
            pltpu.VMEM((HD, 2 * HD), F32),
            pltpu.VMEM((SUBS, HD, 2 * HD), BF16),
            pltpu.VMEM((HD, 2 * HD), BF16),
            pltpu.VMEM((HD, 2 * HD), BF16),
            pltpu.VMEM((X, QUARTER, 2 * HD), F32),
            pltpu.VMEM((2, QUARTER, HD), BF16),
            pltpu.VMEM((Z - 1, QUARTER, HD), BF16),
            pltpu.VMEM((X, QUARTER, HD), F32),
            pltpu.VMEM((X, QUARTER, HD), F32),
            pltpu.SemaphoreType.REGULAR,
            pltpu.SemaphoreType.REGULAR,
            pltpu.SemaphoreType.DMA((8,)),
            pltpu.SemaphoreType.DMA((exchanges,)),
            pltpu.SemaphoreType.DMA((exchanges,)),
            pltpu.SemaphoreType.DMA((len(PARTS), 9)),
            pltpu.SemaphoreType.DMA((len(PARTS), 9)),
        ],
        compiler_params=pltpu.CompilerParams(
            collective_id=0, has_side_effects=True, vmem_limit_bytes=40 * 2**20
        ),
        cost_estimate=pl.CostEstimate(
            flops=2 * ROWS * (8 * HD * COLS + 1024 * HD), bytes_accessed=8 * 2**20, transcendentals=ROWS
        ),
    )(hbm(queries), hbm(keys), hbm(values), prefix, hbm(norm_gain.reshape(1, HD)), hbm(out_weight))


def solution(mesh):
    return jax.shard_map(
        body,
        mesh=mesh,
        in_specs=(
            P("ctx", "head"),
            P("ctx", "head"),
            P("ctx", "head"),
            P(),
            P("head"),
            P(None, "head"),
        ),
        out_specs=P("ctx", "head"),
        check_vma=False,
    )
```

```python
import jax
import jax.numpy as jnp
from jax import lax
from jax.experimental import pallas as pl
from jax.experimental.pallas import tpu as pltpu
from jax.sharding import PartitionSpec as P

MESH = pl.DeviceIdType.MESH
HD = 128
X, Y, Z, CORES = 4, 4, 8, 2
HEADS = Y * CORES
ROWS = 3072
COLS = 512
SUB = 256
SUBS = ROWS // SUB
UNIT = 512
UNITS = ROWS // UNIT
STEPS = UNIT // SUB
AHEAD_Z, EARLY_AHEAD, EARLY_ELSE = 3, 2, 1
GIVEN_AHEAD, GIVEN_ELSE = 2, 2
BESIDE_FIRST = 4
STATE_ROWS = HD + 16
STATE_AT = ROWS + EARLY_AHEAD * UNIT
GAIN_AT = STATE_AT + HD
GATHERED = STATE_AT + STATE_ROWS
LOCALS = UNITS
STATE = UNITS + EARLY_AHEAD
PARTS = [(i * UNIT, UNIT) for i in range(UNITS + EARLY_AHEAD)] + [(STATE_AT, STATE_ROWS)]
DIRECT = (STATE,)
QUARTER = HD // X
NT = (((1,), (1,)), ((), ()))
TN = (((0,), (0,)), ((), ()))
F32, BF16 = jnp.float32, jnp.bfloat16

FROM_LEFT, FROM_RIGHT, FAR_A, FAR_B, SIB_OWN, SIB_LEFT, SIB_RIGHT, SIB_A, SIB_B = range(9)


def split_two(x):
    high = x.astype(BF16)
    return jnp.concatenate([high, (x - high.astype(F32)).astype(BF16)], axis=1)


def dot_two(rows, halves):
    both = jnp.dot(rows, halves, preferred_element_type=F32)
    return both[:, :HD] + both[:, HD:]


def normalize(attended, gain):
    mean_square = jnp.mean(attended * attended, axis=-1, keepdims=True)
    return (attended * lax.rsqrt(mean_square + 1e-06) * gain).astype(BF16)


def kernel(
    q_hbm, k_hbm, v_hbm, prefix_ref, gain_hbm, w_hbm, out,
    q, k, v, w, gain_ref, local, gathered, total, earlier, own_masked, read_state,
    got1, sums, got2, give3, got3,
    near_sem, far_sem, load_sem, ex_send, ex_recv, ring_send, ring_recv,
):
    ctx, head = lax.axis_index("ctx"), lax.axis_index("head")
    z, x = ctx // X, ctx % X
    y, core = head // CORES, head % CORES

    x_peers = [(z * X + (x + s) % X, head) for s in range(1, X)]
    z_peers = [(((z + s) % Z) * X + x, head) for s in range(1, Z)]
    up, down = (y + 1) % Y, (y + Y - 1) % Y
    right, left = (ctx, up * CORES + core), (ctx, down * CORES + core)
    far = (ctx, ((y + 2) % Y) * CORES + core)
    sibling = (ctx, y * CORES + 1 - core)

    barrier = pltpu.get_barrier_semaphore()
    for s in range(1, Y):
        pl.semaphore_signal(
            barrier, inc=1, device_id=(ctx, ((y + s) % Y) * CORES), device_id_type=MESH
        )

    @pl.when(core == 1)
    def _():
        pl.semaphore_signal(barrier, inc=1, device_id=sibling, device_id_type=MESH)

    for peer in x_peers:
        pl.semaphore_signal(barrier, inc=1, device_id=peer, device_id_type=MESH)
    for peer, _ in z_peers:
        pl.semaphore_signal(barrier, inc=1, device_id=(peer, y * CORES + 1), device_id_type=MESH)

    loads = [
        pltpu.make_async_copy(src, dst, load_sem.at[i])
        for i, (src, dst) in enumerate([
            (q_hbm.at[pl.ds(0, EARLY_AHEAD * UNIT)], gathered.at[head, pl.ds(0, EARLY_AHEAD * UNIT)]),
            (q_hbm, q), (gain_hbm, gain_ref), (w_hbm, w),
        ] + [
            (src.at[pl.ds(i * ROWS // 2, ROWS // 2)], dst.at[pl.ds(i * ROWS // 2, ROWS // 2)])
            for i in range(2) for src, dst in ((k_hbm, k), (v_hbm, v))
        ])
    ]
    early_load, q_load, gain_load, w_load = loads[:4]
    ahead = z < AHEAD_Z
    for load in loads[4:]:
        load.start()

    far_head = ((y + 2) % Y) * CORES + core
    left_head, right_head = down * CORES + core, up * CORES + core

    def copy(part, slot):
        start, count = PARTS[part]
        direct = part in DIRECT
        upper = count if direct else (count // 2 + 15) // 16 * 16
        heads, first, count, peer = (
            (head, start, count, right),
            (head, start, count, left),
            (head, start, count, far) if direct else (left_head, start, upper, right),
            (right_head, start + upper, count - upper, left),
            (head, start, count, sibling),
            (left_head, start, count, sibling),
            (right_head, start, count, sibling),
            (far_head, start, upper, sibling),
            (far_head, start + upper, count - upper, sibling),
        )[slot]
        piece = gathered.at[heads, pl.ds(first, count)]
        return pltpu.make_async_remote_copy(
            src_ref=piece, dst_ref=piece,
            send_sem=ring_send.at[part, slot], recv_sem=ring_recv.at[part, slot],
            device_id=peer, device_id_type=MESH,
        )

    def slots(part):
        return [slot for slot in range(9) if part not in DIRECT or slot not in (FAR_B, SIB_B)]

    def give(part):
        if part in DIRECT:
            copy(part, FAR_A).start()
        for slot in (FROM_LEFT, FROM_RIGHT, SIB_OWN):
            copy(part, slot).start()

    def forward(part):
        copy(part, FROM_LEFT).wait_recv()
        if part not in DIRECT:
            copy(part, FAR_A).start()
        copy(part, SIB_LEFT).start()
        copy(part, FROM_RIGHT).wait_recv()
        if part not in DIRECT:
            copy(part, FAR_B).start()
        copy(part, SIB_RIGHT).start()

    def pass_far(part):
        copy(part, FAR_A).wait_recv()
        copy(part, SIB_A).start()
        if part not in DIRECT:
            copy(part, FAR_B).wait_recv()
            copy(part, SIB_B).start()

    def arrived(*parts):
        for part in parts:
            for slot in slots(part):
                if slot >= SIB_OWN:
                    copy(part, slot).wait_recv()

    def meet():
        @pl.when(core == 0)
        def _():
            pl.semaphore_signal(near_sem, inc=1, device_id=sibling, device_id_type=MESH)

        @pl.when(core == 1)
        def _():
            pl.semaphore_wait(near_sem, 1)

    prefix = prefix_ref[0]
    base = ctx * ROWS

    def inside(block):
        at = base + block * SUB + lax.broadcasted_iota(jnp.int32, (SUB, HD), 0)
        return at < prefix

    def state(block, carry):
        rows = pl.ds(block * SUB, SUB)
        vals = v[rows, :]
        masked = jnp.where(inside(block), vals, jnp.zeros_like(vals))
        earlier[block] = split_two(carry[:, :HD])
        return carry + lax.dot_general(
            k[rows, :], jnp.concatenate([vals, masked], axis=1), TN, preferred_element_type=F32
        )

    loads[4].wait()
    loads[5].wait()
    early_load.start()
    q_load.start()
    gain_load.start()
    w_load.start()
    summed = lax.fori_loop(0, SUBS // 2, state, jnp.zeros((HD, 2 * HD), F32))
    loads[6].wait()
    loads[7].wait()
    summed = lax.fori_loop(SUBS // 2, SUBS, state, summed)
    total[...] = summed
    own_masked[...] = split_two(summed[:, HD:])
    mine = pl.ds(pl.multiple_of(x * QUARTER, QUARTER), QUARTER)
    got1[x] = total[mine, :]

    row_at = lax.broadcasted_iota(jnp.int32, (SUB, SUB), 0)
    col_at = lax.broadcasted_iota(jnp.int32, (SUB, SUB), 1)

    def causal(block, _):
        rows = pl.ds(block * SUB, SUB)
        queries = q[rows, :]
        scores = lax.dot_general(queries, k[rows, :], NT, preferred_element_type=F32)
        weights = jnp.where(col_at <= row_at, scores, 0.0).astype(BF16)
        near = jnp.dot(weights, v[rows, :], preferred_element_type=F32)
        near = near + dot_two(queries, earlier[block])
        local[rows, :] = jnp.where(inside(block), dot_two(queries, own_masked[...]), near)
        return 0

    def give_local(unit):
        lax.fori_loop(unit * STEPS, (unit + 1) * STEPS, causal, 0)
        rows = slice(unit * UNIT, (unit + 1) * UNIT)
        gathered[head, ROWS + rows.start:ROWS + rows.stop, :] = local[rows, :].astype(BF16)
        give(LOCALS + unit)

    @pl.when(core == 0)
    def _():
        pl.semaphore_wait(barrier, 1 + (Y - 1) * CORES + X - 1)

    @pl.when(ahead)
    def _():
        meet()
        early_load.wait()
        for unit in range(EARLY_AHEAD):
            give(unit)
        q_load.wait()


    @pl.when(core == 1)
    def _():
        pl.semaphore_wait(barrier, CORES * (Z - 1) + X - 1)

    def exchange(src, dst, slot, peer):
        return pltpu.make_async_remote_copy(
            src_ref=src, dst_ref=dst, send_sem=ex_send.at[slot], recv_sem=ex_recv.at[slot],
            device_id=peer, device_id_type=MESH,
        )

    first = []
    for s in range(1, X):
        quarter = pl.ds(pl.multiple_of(((x + s) % X) * QUARTER, QUARTER), QUARTER)
        first.append(exchange(total.at[quarter], got1.at[x], s - 1, x_peers[s - 1]))
        first[-1].start()

    @pl.when(~ahead)
    def _():
        meet()

    @pl.when(core == 1)
    def _():
        pl.semaphore_signal(far_sem, inc=1, device_id=sibling, device_id_type=MESH)

    @pl.when(ahead)
    def _():
        for unit in range(EARLY_AHEAD):
            give_local(unit)

    @pl.when(~ahead)
    def _():
        early_load.wait()
        for unit in range(EARLY_ELSE):
            give(unit)
        q_load.wait()
        for unit in range(EARLY_ELSE):
            give_local(unit)
        lax.fori_loop(EARLY_ELSE * STEPS, BESIDE_FIRST, causal, 0)

    for moved in first:
        moved.wait_recv()
    along_x = got1[0] + got1[1] + got1[2] + got1[3]
    sums[0] = along_x[:, :HD].astype(BF16)
    sums[1] = along_x[:, HD:].astype(BF16)

    @pl.when(core == 0)
    def _():
        pl.semaphore_wait(far_sem, 1)

    second = []
    for s in range(1, Z):
        second.append(exchange(sums.at[(z + s) // Z], got2.at[s - 1], X - 2 + s, z_peers[s - 1]))
        second[-1].start()

    @pl.when(ahead)
    def _():
        forward(0)
        lax.fori_loop(EARLY_AHEAD * STEPS, SUBS, causal, 0)
        forward(1)

    @pl.when(~ahead)
    def _():
        lax.fori_loop(BESIDE_FIRST, SUBS, causal, 0)
        forward(0)

    for moved in second:
        moved.wait_recv()
    along_z = got2[0].astype(F32)
    for s in range(1, Z - 1):
        along_z = along_z + got2[s].astype(F32)
    for to in range(X):
        part = along_z
        for s in range(X):
            if s < to:
                part = part + got1[s][:, :HD]
            elif s > to:
                part = part + got1[s][:, HD:]
        give3[to] = part
    got3[x] = give3[x]

    third = []
    for s in range(1, X):
        third.append(exchange(give3.at[(x + s) % X], got3.at[x], X + Z - 3 + s, x_peers[s - 1]))
        third[-1].start()

    @pl.when(ahead)
    def _():
        forward(LOCALS)
        forward(LOCALS + 1)

    @pl.when(~ahead)
    def _():
        forward(LOCALS)

    for moved in third:
        moved.wait_recv()
    read_state[...] = split_two(got3[...].reshape(HD, HD))

    gain_load.wait()
    gain = gain_ref[...]

    def give_state():
        gathered[head, STATE_AT:GAIN_AT, :] = read_state[:, :HD]
        gain_high = gain.astype(BF16).astype(F32)
        gain_row = lax.broadcasted_iota(jnp.int32, (16, HD), 0)
        gathered[head, GAIN_AT:GATHERED, :] = jnp.where(
            gain_row == 0, gain_high, jnp.where(gain_row == 1, gain - gain_high, 0.0)
        ).astype(BF16)
        give(STATE)

    def norm(unit):
        rows = slice(unit * UNIT, (unit + 1) * UNIT)
        attended = dot_two(q[rows, :], read_state[...]) + local[rows, :]
        gathered[head, rows, :] = normalize(attended, gain)
        give(unit)

    def project(unit):
        def one(step, _):
            rows = pl.ds(pl.multiple_of(step * SUB, SUB), SUB)
            normed = jnp.concatenate([gathered[h, rows, :] for h in range(HEADS)], axis=1)
            out[rows, :] = jnp.dot(normed, w[...], preferred_element_type=F32).astype(BF16)
            return 0

        lax.fori_loop(unit * STEPS, (unit + 1) * STEPS, one, 0)

    def early(step, _):
        rows = pl.ds(pl.multiple_of(step * SUB, SUB), SUB)
        local_rows = pl.ds(pl.multiple_of(ROWS + step * SUB, SUB), SUB)
        normed = []
        for h in range(HEADS):
            gains = gathered[h, GAIN_AT:GATHERED, :].astype(F32)
            attended = jnp.dot(
                gathered[h, rows, :], gathered[h, STATE_AT:GAIN_AT, :], preferred_element_type=F32
            ) + gathered[h, local_rows, :].astype(F32)
            normed.append(normalize(attended, gains[0:1] + gains[1:2]))
        out[rows, :] = jnp.dot(
            jnp.concatenate(normed, axis=1), w[...], preferred_element_type=F32
        ).astype(BF16)
        return 0

    w_load.wait()

    def drain(part, which=range(9)):
        for slot in slots(part):
            if slot in which:
                copy(part, slot).wait_send()

    def finish(early_units, given):
        units = list(range(early_units, UNITS))
        before = [part for unit in range(early_units) for part in (unit, LOCALS + unit)]
        give_state()
        for unit in units[:given]:
            norm(unit)
        for part in before:
            pass_far(part)
        forward(STATE)
        pass_far(STATE)
        arrived(STATE)
        sent = before + [STATE]
        for i, unit in enumerate(units):
            if i < early_units:
                arrived(i, LOCALS + i)
                lax.fori_loop(i * STEPS, (i + 1) * STEPS, early, 0)
            if i + given < len(units):
                norm(units[i + given])
            forward(unit)
            if i > 1:
                arrived(units[i - 2])
                project(units[i - 2])
            if i > 0:
                pass_far(units[i - 1])
                for part in sent[:2]:
                    drain(part)
                sent = sent[2:]
            else:
                for moved in first + second + third:
                    moved.wait_send()
        for part in sent + units[:-2]:
            drain(part)
        arrived(units[-2])
        project(units[-2])
        pass_far(units[-1])
        drain(units[-2])
        drain(units[-1], range(SIB_A))
        arrived(units[-1])
        project(units[-1])
        drain(units[-1], (SIB_A, SIB_B))

    @pl.when(ahead)
    def _():
        finish(EARLY_AHEAD, GIVEN_AHEAD)

    @pl.when(~ahead)
    def _():
        finish(EARLY_ELSE, GIVEN_ELSE)


def body(queries, keys, values, prefix, norm_gain, out_weight):
    def hbm(array):
        return pltpu.with_memory_space_constraint(array, pltpu.HBM)

    anywhere = pl.BlockSpec(memory_space=pl.ANY)
    exchanges = 2 * (X - 1) + Z - 1
    return pl.pallas_call(
        kernel,
        out_shape=pltpu.VMEM((ROWS, COLS), BF16),
        in_specs=[
            anywhere, anywhere, anywhere,
            pl.BlockSpec(memory_space=pltpu.SMEM),
            anywhere, anywhere,
        ],
        out_specs=pl.BlockSpec(memory_space=pltpu.VMEM),
        scratch_shapes=[
            pltpu.VMEM((ROWS, HD), BF16),
            pltpu.VMEM((ROWS, HD), BF16),
            pltpu.VMEM((ROWS, HD), BF16),
            pltpu.VMEM((HEADS * HD, COLS), BF16),
            pltpu.VMEM((1, HD), F32),
            pltpu.VMEM((ROWS, HD), F32),
            pltpu.VMEM((HEADS, GATHERED, HD), BF16),
            pltpu.VMEM((HD, 2 * HD), F32),
            pltpu.VMEM((SUBS, HD, 2 * HD), BF16),
            pltpu.VMEM((HD, 2 * HD), BF16),
            pltpu.VMEM((HD, 2 * HD), BF16),
            pltpu.VMEM((X, QUARTER, 2 * HD), F32),
            pltpu.VMEM((2, QUARTER, HD), BF16),
            pltpu.VMEM((Z - 1, QUARTER, HD), BF16),
            pltpu.VMEM((X, QUARTER, HD), F32),
            pltpu.VMEM((X, QUARTER, HD), F32),
            pltpu.SemaphoreType.REGULAR,
            pltpu.SemaphoreType.REGULAR,
            pltpu.SemaphoreType.DMA((8,)),
            pltpu.SemaphoreType.DMA((exchanges,)),
            pltpu.SemaphoreType.DMA((exchanges,)),
            pltpu.SemaphoreType.DMA((len(PARTS), 9)),
            pltpu.SemaphoreType.DMA((len(PARTS), 9)),
        ],
        compiler_params=pltpu.CompilerParams(
            collective_id=0, has_side_effects=True, vmem_limit_bytes=40 * 2**20
        ),
        cost_estimate=pl.CostEstimate(
            flops=2 * ROWS * (8 * HD * COLS + 1024 * HD), bytes_accessed=8 * 2**20, transcendentals=ROWS
        ),
    )(hbm(queries), hbm(keys), hbm(values), prefix, hbm(norm_gain.reshape(1, HD)), hbm(out_weight))


def solution(mesh):
    return jax.shard_map(
        body,
        mesh=mesh,
        in_specs=(
            P("ctx", "head"),
            P("ctx", "head"),
            P("ctx", "head"),
            P(),
            P("head"),
            P(None, "head"),
        ),
        out_specs=P("ctx", "head"),
        check_vma=False,
    )
```

```python
import jax
import jax.numpy as jnp
from jax import lax
from jax.experimental import pallas as pl
from jax.experimental.pallas import tpu as pltpu
from jax.sharding import PartitionSpec as P

MESH = pl.DeviceIdType.MESH
HD = 128
X, Y, Z, CORES = 4, 4, 8, 2
HEADS = Y * CORES
ROWS = 3072
COLS = 512
SUB = 256
SUBS = ROWS // SUB
UNIT = 512
UNITS = ROWS // UNIT
STEPS = UNIT // SUB
AHEAD_Z, EARLY_AHEAD, EARLY_ELSE = 3, 2, 1
GIVEN_AHEAD, GIVEN_ELSE = 2, 2
BESIDE_FIRST = 4
STATE_ROWS = HD + 16
STATE_AT = ROWS + EARLY_AHEAD * UNIT
GAIN_AT = STATE_AT + HD
GATHERED = STATE_AT + STATE_ROWS
LOCALS = UNITS
STATE = UNITS + EARLY_AHEAD
PARTS = [(i * UNIT, UNIT) for i in range(UNITS + EARLY_AHEAD)] + [(STATE_AT, STATE_ROWS)]
DIRECT = (STATE,)
QUARTER = HD // X
NT = (((1,), (1,)), ((), ()))
TN = (((0,), (0,)), ((), ()))
F32, BF16 = jnp.float32, jnp.bfloat16

FROM_LEFT, FROM_RIGHT, FAR_A, FAR_B, SIB_OWN, SIB_LEFT, SIB_RIGHT, SIB_A, SIB_B = range(9)


def split_two(x):
    high = x.astype(BF16)
    return jnp.concatenate([high, (x - high.astype(F32)).astype(BF16)], axis=1)


def dot_two(rows, halves):
    both = jnp.dot(rows, halves, preferred_element_type=F32)
    return both[:, :HD] + both[:, HD:]


def normalize(attended, gain):
    mean_square = jnp.mean(attended * attended, axis=-1, keepdims=True)
    return (attended * lax.rsqrt(mean_square + 1e-06) * gain).astype(BF16)


def kernel(
    q_hbm, k_hbm, v_hbm, prefix_ref, gain_hbm, w_hbm, out,
    q, k, v, w, gain_ref, local, gathered, total, earlier, own_masked, read_state,
    got1, sums, got2, give3, got3,
    near_sem, far_sem, load_sem, ex_send, ex_recv, ring_send, ring_recv,
):
    ctx, head = lax.axis_index("ctx"), lax.axis_index("head")
    z, x = ctx // X, ctx % X
    y, core = head // CORES, head % CORES

    x_peers = [(z * X + (x + s) % X, head) for s in range(1, X)]
    z_peers = [(((z + s) % Z) * X + x, head) for s in range(1, Z)]
    up, down = (y + 1) % Y, (y + Y - 1) % Y
    right, left = (ctx, up * CORES + core), (ctx, down * CORES + core)
    far = (ctx, ((y + 2) % Y) * CORES + core)
    sibling = (ctx, y * CORES + 1 - core)

    barrier = pltpu.get_barrier_semaphore()
    for s in range(1, Y):
        pl.semaphore_signal(
            barrier, inc=1, device_id=(ctx, ((y + s) % Y) * CORES), device_id_type=MESH
        )

    @pl.when(core == 1)
    def _():
        pl.semaphore_signal(barrier, inc=1, device_id=sibling, device_id_type=MESH)

    for peer in x_peers:
        pl.semaphore_signal(barrier, inc=1, device_id=peer, device_id_type=MESH)
    for peer, _ in z_peers:
        pl.semaphore_signal(barrier, inc=1, device_id=(peer, y * CORES + 1), device_id_type=MESH)

    loads = [
        pltpu.make_async_copy(src, dst, load_sem.at[i])
        for i, (src, dst) in enumerate([
            (q_hbm.at[pl.ds(0, EARLY_AHEAD * UNIT)], gathered.at[head, pl.ds(0, EARLY_AHEAD * UNIT)]),
            (q_hbm, q), (gain_hbm, gain_ref), (w_hbm, w),
        ] + [
            (src.at[pl.ds(i * ROWS // 2, ROWS // 2)], dst.at[pl.ds(i * ROWS // 2, ROWS // 2)])
            for i in range(2) for src, dst in ((k_hbm, k), (v_hbm, v))
        ])
    ]
    early_load, q_load, gain_load, w_load = loads[:4]
    ahead = z < AHEAD_Z
    for load in loads[4:]:
        load.start()

    far_head = ((y + 2) % Y) * CORES + core
    left_head, right_head = down * CORES + core, up * CORES + core

    def copy(part, slot):
        start, count = PARTS[part]
        direct = part in DIRECT
        upper = count if direct else (count // 2 + 15) // 16 * 16
        heads, first, count, peer = (
            (head, start, count, right),
            (head, start, count, left),
            (head, start, count, far) if direct else (left_head, start, upper, right),
            (right_head, start + upper, count - upper, left),
            (head, start, count, sibling),
            (left_head, start, count, sibling),
            (right_head, start, count, sibling),
            (far_head, start, upper, sibling),
            (far_head, start + upper, count - upper, sibling),
        )[slot]
        piece = gathered.at[heads, pl.ds(first, count)]
        return pltpu.make_async_remote_copy(
            src_ref=piece, dst_ref=piece,
            send_sem=ring_send.at[part, slot], recv_sem=ring_recv.at[part, slot],
            device_id=peer, device_id_type=MESH,
        )

    def slots(part):
        return [slot for slot in range(9) if part not in DIRECT or slot not in (FAR_B, SIB_B)]

    def give(part):
        if part in DIRECT:
            copy(part, FAR_A).start()
        for slot in (FROM_LEFT, FROM_RIGHT, SIB_OWN):
            copy(part, slot).start()

    def forward(part):
        copy(part, FROM_LEFT).wait_recv()
        if part not in DIRECT:
            copy(part, FAR_A).start()
        copy(part, SIB_LEFT).start()
        copy(part, FROM_RIGHT).wait_recv()
        if part not in DIRECT:
            copy(part, FAR_B).start()
        copy(part, SIB_RIGHT).start()

    def pass_far(part):
        copy(part, FAR_A).wait_recv()
        copy(part, SIB_A).start()
        if part not in DIRECT:
            copy(part, FAR_B).wait_recv()
            copy(part, SIB_B).start()

    def arrived(*parts):
        for part in parts:
            for slot in slots(part):
                if slot >= SIB_OWN:
                    copy(part, slot).wait_recv()

    def meet():
        @pl.when(core == 0)
        def _():
            pl.semaphore_signal(near_sem, inc=1, device_id=sibling, device_id_type=MESH)

        @pl.when(core == 1)
        def _():
            pl.semaphore_wait(near_sem, 1)

    prefix = prefix_ref[0]
    base = ctx * ROWS

    def inside(block):
        at = base + block * SUB + lax.broadcasted_iota(jnp.int32, (SUB, HD), 0)
        return at < prefix

    def state(block, carry):
        rows = pl.ds(block * SUB, SUB)
        vals = v[rows, :]
        masked = jnp.where(inside(block), vals, jnp.zeros_like(vals))
        earlier[block] = split_two(carry[:, :HD])
        return carry + lax.dot_general(
            k[rows, :], jnp.concatenate([vals, masked], axis=1), TN, preferred_element_type=F32
        )

    loads[4].wait()
    loads[5].wait()
    early_load.start()
    q_load.start()
    gain_load.start()
    w_load.start()
    summed = lax.fori_loop(0, SUBS // 2, state, jnp.zeros((HD, 2 * HD), F32))
    loads[6].wait()
    loads[7].wait()
    summed = lax.fori_loop(SUBS // 2, SUBS, state, summed)
    total[...] = summed
    own_masked[...] = split_two(summed[:, HD:])
    mine = pl.ds(pl.multiple_of(x * QUARTER, QUARTER), QUARTER)
    got1[x] = total[mine, :]

    row_at = lax.broadcasted_iota(jnp.int32, (SUB, SUB), 0)
    col_at = lax.broadcasted_iota(jnp.int32, (SUB, SUB), 1)

    def causal(block, _):
        rows = pl.ds(block * SUB, SUB)
        queries = q[rows, :]
        scores = lax.dot_general(queries, k[rows, :], NT, preferred_element_type=F32)
        weights = jnp.where(col_at <= row_at, scores, 0.0).astype(BF16)
        near = jnp.dot(weights, v[rows, :], preferred_element_type=F32)
        near = near + dot_two(queries, earlier[block])
        local[rows, :] = jnp.where(inside(block), dot_two(queries, own_masked[...]), near)
        return 0

    def give_local(unit):
        lax.fori_loop(unit * STEPS, (unit + 1) * STEPS, causal, 0)
        rows = slice(unit * UNIT, (unit + 1) * UNIT)
        gathered[head, ROWS + rows.start:ROWS + rows.stop, :] = local[rows, :].astype(BF16)
        give(LOCALS + unit)

    @pl.when(core == 0)
    def _():
        pl.semaphore_wait(barrier, 1 + (Y - 1) * CORES + X - 1)

    @pl.when(ahead)
    def _():
        meet()
        early_load.wait()
        for unit in range(EARLY_AHEAD):
            give(unit)
        q_load.wait()


    @pl.when(core == 1)
    def _():
        pl.semaphore_wait(barrier, CORES * (Z - 1) + X - 1)

    def exchange(src, dst, slot, peer):
        return pltpu.make_async_remote_copy(
            src_ref=src, dst_ref=dst, send_sem=ex_send.at[slot], recv_sem=ex_recv.at[slot],
            device_id=peer, device_id_type=MESH,
        )

    first = []
    for s in range(1, X):
        quarter = pl.ds(pl.multiple_of(((x + s) % X) * QUARTER, QUARTER), QUARTER)
        first.append(exchange(total.at[quarter], got1.at[x], s - 1, x_peers[s - 1]))
        first[-1].start()

    @pl.when(~ahead)
    def _():
        meet()

    @pl.when(core == 1)
    def _():
        pl.semaphore_signal(far_sem, inc=1, device_id=sibling, device_id_type=MESH)

    @pl.when(ahead)
    def _():
        for unit in range(EARLY_AHEAD):
            give_local(unit)

    @pl.when(~ahead)
    def _():
        early_load.wait()
        for unit in range(EARLY_ELSE):
            give(unit)
        q_load.wait()
        for unit in range(EARLY_ELSE):
            give_local(unit)
        lax.fori_loop(EARLY_ELSE * STEPS, BESIDE_FIRST, causal, 0)

    for moved in first:
        moved.wait_recv()
    along_x = got1[0] + got1[1] + got1[2] + got1[3]
    sums[0] = along_x[:, :HD].astype(BF16)
    sums[1] = along_x[:, HD:].astype(BF16)

    @pl.when(core == 0)
    def _():
        pl.semaphore_wait(far_sem, 1)

    second = []
    for s in range(1, Z):
        second.append(exchange(sums.at[(z + s) // Z], got2.at[s - 1], X - 2 + s, z_peers[s - 1]))
        second[-1].start()

    @pl.when(ahead)
    def _():
        forward(0)
        lax.fori_loop(EARLY_AHEAD * STEPS, SUBS, causal, 0)
        forward(1)

    @pl.when(~ahead)
    def _():
        lax.fori_loop(BESIDE_FIRST, SUBS, causal, 0)
        forward(0)

    for moved in second:
        moved.wait_recv()
    along_z = got2[0].astype(F32)
    for s in range(1, Z - 1):
        along_z = along_z + got2[s].astype(F32)
    for to in range(X):
        part = along_z
        for s in range(X):
            if s < to:
                part = part + got1[s][:, :HD]
            elif s > to:
                part = part + got1[s][:, HD:]
        give3[to] = part
    got3[x] = give3[x]

    third = []
    for s in range(1, X):
        third.append(exchange(give3.at[(x + s) % X], got3.at[x], X + Z - 3 + s, x_peers[s - 1]))
        third[-1].start()

    @pl.when(ahead)
    def _():
        forward(LOCALS)
        forward(LOCALS + 1)

    @pl.when(~ahead)
    def _():
        forward(LOCALS)

    for moved in third:
        moved.wait_recv()
    read_state[...] = split_two(got3[...].reshape(HD, HD))

    gain_load.wait()
    gain = gain_ref[...]

    def give_state():
        gathered[head, STATE_AT:GAIN_AT, :] = read_state[:, :HD]
        gain_high = gain.astype(BF16).astype(F32)
        gain_row = lax.broadcasted_iota(jnp.int32, (16, HD), 0)
        gathered[head, GAIN_AT:GATHERED, :] = jnp.where(
            gain_row == 0, gain_high, jnp.where(gain_row == 1, gain - gain_high, 0.0)
        ).astype(BF16)
        give(STATE)

    def norm(unit):
        rows = slice(unit * UNIT, (unit + 1) * UNIT)
        attended = dot_two(q[rows, :], read_state[...]) + local[rows, :]
        gathered[head, rows, :] = normalize(attended, gain)
        give(unit)

    def project(unit):
        def one(step, _):
            rows = pl.ds(pl.multiple_of(step * SUB, SUB), SUB)
            normed = jnp.concatenate([gathered[h, rows, :] for h in range(HEADS)], axis=1)
            out[rows, :] = jnp.dot(normed, w[...], preferred_element_type=F32).astype(BF16)
            return 0

        lax.fori_loop(unit * STEPS, (unit + 1) * STEPS, one, 0)

    def early(step, _):
        rows = pl.ds(pl.multiple_of(step * SUB, SUB), SUB)
        local_rows = pl.ds(pl.multiple_of(ROWS + step * SUB, SUB), SUB)
        normed = []
        for h in range(HEADS):
            gains = gathered[h, GAIN_AT:GATHERED, :].astype(F32)
            attended = jnp.dot(
                gathered[h, rows, :], gathered[h, STATE_AT:GAIN_AT, :], preferred_element_type=F32
            ) + gathered[h, local_rows, :].astype(F32)
            normed.append(normalize(attended, gains[0:1] + gains[1:2]))
        out[rows, :] = jnp.dot(
            jnp.concatenate(normed, axis=1), w[...], preferred_element_type=F32
        ).astype(BF16)
        return 0

    w_load.wait()

    def drain(part, which=range(9)):
        for slot in slots(part):
            if slot in which:
                copy(part, slot).wait_send()

    def finish(early_units, given):
        units = list(range(early_units, UNITS))
        before = [part for unit in range(early_units) for part in (unit, LOCALS + unit)]
        give_state()
        for unit in units[:given]:
            norm(unit)
        for part in before:
            pass_far(part)
        forward(STATE)
        pass_far(STATE)
        arrived(STATE)
        sent = before + [STATE]
        for i, unit in enumerate(units):
            if i < early_units:
                arrived(i, LOCALS + i)
                lax.fori_loop(i * STEPS, (i + 1) * STEPS, early, 0)
            if i + given < len(units):
                norm(units[i + given])
            forward(unit)
            if i > 1:
                pass_far(units[i - 2])
            if i > 2:
                arrived(units[i - 3])
                project(units[i - 3])
            if i > 0:
                for part in sent[:2]:
                    drain(part)
                sent = sent[2:]
            else:
                for moved in first + second + third:
                    moved.wait_send()
        pass_far(units[-2])
        for part in sent + units[:-2]:
            drain(part)
        arrived(units[-3])
        project(units[-3])
        arrived(units[-2])
        project(units[-2])
        pass_far(units[-1])
        drain(units[-2])
        drain(units[-1], range(SIB_A))
        arrived(units[-1])
        project(units[-1])
        drain(units[-1], (SIB_A, SIB_B))

    @pl.when(ahead)
    def _():
        finish(EARLY_AHEAD, GIVEN_AHEAD)

    @pl.when(~ahead)
    def _():
        finish(EARLY_ELSE, GIVEN_ELSE)


def body(queries, keys, values, prefix, norm_gain, out_weight):
    def hbm(array):
        return pltpu.with_memory_space_constraint(array, pltpu.HBM)

    anywhere = pl.BlockSpec(memory_space=pl.ANY)
    exchanges = 2 * (X - 1) + Z - 1
    return pl.pallas_call(
        kernel,
        out_shape=pltpu.VMEM((ROWS, COLS), BF16),
        in_specs=[
            anywhere, anywhere, anywhere,
            pl.BlockSpec(memory_space=pltpu.SMEM),
            anywhere, anywhere,
        ],
        out_specs=pl.BlockSpec(memory_space=pltpu.VMEM),
        scratch_shapes=[
            pltpu.VMEM((ROWS, HD), BF16),
            pltpu.VMEM((ROWS, HD), BF16),
            pltpu.VMEM((ROWS, HD), BF16),
            pltpu.VMEM((HEADS * HD, COLS), BF16),
            pltpu.VMEM((1, HD), F32),
            pltpu.VMEM((ROWS, HD), F32),
            pltpu.VMEM((HEADS, GATHERED, HD), BF16),
            pltpu.VMEM((HD, 2 * HD), F32),
            pltpu.VMEM((SUBS, HD, 2 * HD), BF16),
            pltpu.VMEM((HD, 2 * HD), BF16),
            pltpu.VMEM((HD, 2 * HD), BF16),
            pltpu.VMEM((X, QUARTER, 2 * HD), F32),
            pltpu.VMEM((2, QUARTER, HD), BF16),
            pltpu.VMEM((Z - 1, QUARTER, HD), BF16),
            pltpu.VMEM((X, QUARTER, HD), F32),
            pltpu.VMEM((X, QUARTER, HD), F32),
            pltpu.SemaphoreType.REGULAR,
            pltpu.SemaphoreType.REGULAR,
            pltpu.SemaphoreType.DMA((8,)),
            pltpu.SemaphoreType.DMA((exchanges,)),
            pltpu.SemaphoreType.DMA((exchanges,)),
            pltpu.SemaphoreType.DMA((len(PARTS), 9)),
            pltpu.SemaphoreType.DMA((len(PARTS), 9)),
        ],
        compiler_params=pltpu.CompilerParams(
            collective_id=0, has_side_effects=True, vmem_limit_bytes=40 * 2**20
        ),
        cost_estimate=pl.CostEstimate(
            flops=2 * ROWS * (8 * HD * COLS + 1024 * HD), bytes_accessed=8 * 2**20, transcendentals=ROWS
        ),
    )(hbm(queries), hbm(keys), hbm(values), prefix, hbm(norm_gain.reshape(1, HD)), hbm(out_weight))


def solution(mesh):
    return jax.shard_map(
        body,
        mesh=mesh,
        in_specs=(
            P("ctx", "head"),
            P("ctx", "head"),
            P("ctx", "head"),
            P(),
            P("head"),
            P(None, "head"),
        ),
        out_specs=P("ctx", "head"),
        check_vma=False,
    )
```

```python
import jax
import jax.numpy as jnp
from jax import lax
from jax.experimental import pallas as pl
from jax.experimental.pallas import tpu as pltpu
from jax.sharding import PartitionSpec as P

MESH = pl.DeviceIdType.MESH
HD = 128
X, Y, Z, CORES = 4, 4, 8, 2
HEADS = Y * CORES
ROWS = 3072
COLS = 512
SUB = 256
SUBS = ROWS // SUB
UNIT = 512
UNITS = ROWS // UNIT
STEPS = UNIT // SUB
AHEAD_Z, EARLY_AHEAD, EARLY_ELSE = 3, 2, 1
GIVEN_AHEAD, GIVEN_ELSE = 2, 2
BESIDE_FIRST = 4
STATE_ROWS = HD + 16
STATE_AT = ROWS + EARLY_AHEAD * UNIT
GAIN_AT = STATE_AT + HD
GATHERED = STATE_AT + STATE_ROWS
LOCALS = UNITS
STATE = UNITS + EARLY_AHEAD
PARTS = [(i * UNIT, UNIT) for i in range(UNITS + EARLY_AHEAD)] + [(STATE_AT, STATE_ROWS)]
DIRECT = (STATE,)
QUARTER = HD // X
NT = (((1,), (1,)), ((), ()))
TN = (((0,), (0,)), ((), ()))
F32, BF16 = jnp.float32, jnp.bfloat16

FROM_LEFT, FROM_RIGHT, FAR_A, FAR_B, SIB_OWN, SIB_LEFT, SIB_RIGHT, SIB_A, SIB_B = range(9)


def split_two(x):
    high = x.astype(BF16)
    return jnp.concatenate([high, (x - high.astype(F32)).astype(BF16)], axis=1)


def dot_two(rows, halves):
    both = jnp.dot(rows, halves, preferred_element_type=F32)
    return both[:, :HD] + both[:, HD:]


def normalize(attended, gain):
    mean_square = jnp.mean(attended * attended, axis=-1, keepdims=True)
    return (attended * lax.rsqrt(mean_square + 1e-06) * gain).astype(BF16)


def kernel(
    q_hbm, k_hbm, v_hbm, prefix_ref, gain_hbm, w_hbm, out,
    q, k, v, w, gain_ref, local, gathered, total, earlier, own_masked, read_state,
    got1, sums, got2, give3, got3,
    near_sem, far_sem, load_sem, ex_send, ex_recv, ring_send, ring_recv,
):
    ctx, head = lax.axis_index("ctx"), lax.axis_index("head")
    z, x = ctx // X, ctx % X
    y, core = head // CORES, head % CORES

    x_peers = [(z * X + (x + s) % X, head) for s in range(1, X)]
    z_peers = [(((z + s) % Z) * X + x, head) for s in range(1, Z)]
    up, down = (y + 1) % Y, (y + Y - 1) % Y
    right, left = (ctx, up * CORES + core), (ctx, down * CORES + core)
    far = (ctx, ((y + 2) % Y) * CORES + core)
    sibling = (ctx, y * CORES + 1 - core)

    barrier = pltpu.get_barrier_semaphore()
    for s in range(1, Y):
        pl.semaphore_signal(
            barrier, inc=1, device_id=(ctx, ((y + s) % Y) * CORES), device_id_type=MESH
        )

    @pl.when(core == 1)
    def _():
        pl.semaphore_signal(barrier, inc=1, device_id=sibling, device_id_type=MESH)

    for peer in x_peers:
        pl.semaphore_signal(barrier, inc=1, device_id=peer, device_id_type=MESH)
    for peer, _ in z_peers:
        pl.semaphore_signal(barrier, inc=1, device_id=(peer, y * CORES + 1), device_id_type=MESH)

    loads = [
        pltpu.make_async_copy(src, dst, load_sem.at[i])
        for i, (src, dst) in enumerate([
            (q_hbm.at[pl.ds(0, EARLY_AHEAD * UNIT)], gathered.at[head, pl.ds(0, EARLY_AHEAD * UNIT)]),
            (q_hbm, q), (gain_hbm, gain_ref), (w_hbm, w),
        ] + [
            (src.at[pl.ds(i * ROWS // 2, ROWS // 2)], dst.at[pl.ds(i * ROWS // 2, ROWS // 2)])
            for i in range(2) for src, dst in ((k_hbm, k), (v_hbm, v))
        ])
    ]
    early_load, q_load, gain_load, w_load = loads[:4]
    ahead = z < AHEAD_Z
    for load in loads[4:]:
        load.start()

    far_head = ((y + 2) % Y) * CORES + core
    left_head, right_head = down * CORES + core, up * CORES + core

    def copy(part, slot):
        start, count = PARTS[part]
        direct = part in DIRECT
        upper = count if direct else (count // 2 + 15) // 16 * 16
        heads, first, count, peer = (
            (head, start, count, right),
            (head, start, count, left),
            (head, start, count, far) if direct else (left_head, start, upper, right),
            (right_head, start + upper, count - upper, left),
            (head, start, count, sibling),
            (left_head, start, count, sibling),
            (right_head, start, count, sibling),
            (far_head, start, upper, sibling),
            (far_head, start + upper, count - upper, sibling),
        )[slot]
        piece = gathered.at[heads, pl.ds(first, count)]
        return pltpu.make_async_remote_copy(
            src_ref=piece, dst_ref=piece,
            send_sem=ring_send.at[part, slot], recv_sem=ring_recv.at[part, slot],
            device_id=peer, device_id_type=MESH,
        )

    def slots(part):
        return [slot for slot in range(9) if part not in DIRECT or slot not in (FAR_B, SIB_B)]

    def give(part):
        if part in DIRECT:
            copy(part, FAR_A).start()
        for slot in (FROM_LEFT, FROM_RIGHT, SIB_OWN):
            copy(part, slot).start()

    def forward(part):
        copy(part, FROM_LEFT).wait_recv()
        if part not in DIRECT:
            copy(part, FAR_A).start()
        copy(part, SIB_LEFT).start()
        copy(part, FROM_RIGHT).wait_recv()
        if part not in DIRECT:
            copy(part, FAR_B).start()
        copy(part, SIB_RIGHT).start()

    def pass_far(part):
        copy(part, FAR_A).wait_recv()
        copy(part, SIB_A).start()
        if part not in DIRECT:
            copy(part, FAR_B).wait_recv()
            copy(part, SIB_B).start()

    def arrived(*parts):
        for part in parts:
            for slot in slots(part):
                if slot >= SIB_OWN:
                    copy(part, slot).wait_recv()

    def meet():
        @pl.when(core == 0)
        def _():
            pl.semaphore_signal(near_sem, inc=1, device_id=sibling, device_id_type=MESH)

        @pl.when(core == 1)
        def _():
            pl.semaphore_wait(near_sem, 1)

    prefix = prefix_ref[0]
    base = ctx * ROWS

    def inside(block):
        at = base + block * SUB + lax.broadcasted_iota(jnp.int32, (SUB, HD), 0)
        return at < prefix

    def state(block, carry):
        rows = pl.ds(block * SUB, SUB)
        vals = v[rows, :]
        masked = jnp.where(inside(block), vals, jnp.zeros_like(vals))
        earlier[block] = split_two(carry[:, :HD])
        return carry + lax.dot_general(
            k[rows, :], jnp.concatenate([vals, masked], axis=1), TN, preferred_element_type=F32
        )

    loads[4].wait()
    loads[5].wait()
    early_load.start()
    q_load.start()
    gain_load.start()
    w_load.start()
    summed = lax.fori_loop(0, SUBS // 2, state, jnp.zeros((HD, 2 * HD), F32))
    loads[6].wait()
    loads[7].wait()
    summed = lax.fori_loop(SUBS // 2, SUBS, state, summed)
    total[...] = summed
    own_masked[...] = split_two(summed[:, HD:])
    mine = pl.ds(pl.multiple_of(x * QUARTER, QUARTER), QUARTER)
    got1[x] = total[mine, :]

    row_at = lax.broadcasted_iota(jnp.int32, (SUB, SUB), 0)
    col_at = lax.broadcasted_iota(jnp.int32, (SUB, SUB), 1)

    def causal(block, _):
        rows = pl.ds(block * SUB, SUB)
        queries = q[rows, :]
        scores = lax.dot_general(queries, k[rows, :], NT, preferred_element_type=F32)
        weights = jnp.where(col_at <= row_at, scores, 0.0).astype(BF16)
        near = jnp.dot(weights, v[rows, :], preferred_element_type=F32)
        near = near + dot_two(queries, earlier[block])
        local[rows, :] = jnp.where(inside(block), dot_two(queries, own_masked[...]), near)
        return 0

    def give_local(unit):
        lax.fori_loop(unit * STEPS, (unit + 1) * STEPS, causal, 0)
        rows = slice(unit * UNIT, (unit + 1) * UNIT)
        gathered[head, ROWS + rows.start:ROWS + rows.stop, :] = local[rows, :].astype(BF16)
        give(LOCALS + unit)

    @pl.when(core == 0)
    def _():
        pl.semaphore_wait(barrier, 1 + (Y - 1) * CORES + X - 1)

    @pl.when(ahead)
    def _():
        meet()
        early_load.wait()
        for unit in range(EARLY_AHEAD):
            give(unit)
        q_load.wait()


    @pl.when(core == 1)
    def _():
        pl.semaphore_wait(barrier, CORES * (Z - 1) + X - 1)

    def exchange(src, dst, slot, peer):
        return pltpu.make_async_remote_copy(
            src_ref=src, dst_ref=dst, send_sem=ex_send.at[slot], recv_sem=ex_recv.at[slot],
            device_id=peer, device_id_type=MESH,
        )

    first = []
    for s in range(1, X):
        quarter = pl.ds(pl.multiple_of(((x + s) % X) * QUARTER, QUARTER), QUARTER)
        first.append(exchange(total.at[quarter], got1.at[x], s - 1, x_peers[s - 1]))
        first[-1].start()

    @pl.when(~ahead)
    def _():
        meet()

    @pl.when(core == 1)
    def _():
        pl.semaphore_signal(far_sem, inc=1, device_id=sibling, device_id_type=MESH)

    @pl.when(ahead)
    def _():
        for unit in range(EARLY_AHEAD):
            give_local(unit)

    @pl.when(~ahead)
    def _():
        early_load.wait()
        for unit in range(EARLY_ELSE):
            give(unit)
        q_load.wait()
        for unit in range(EARLY_ELSE):
            give_local(unit)
        lax.fori_loop(EARLY_ELSE * STEPS, BESIDE_FIRST, causal, 0)

    for moved in first:
        moved.wait_recv()
    along_x = got1[0] + got1[1] + got1[2] + got1[3]
    sums[0] = along_x[:, :HD].astype(BF16)
    sums[1] = along_x[:, HD:].astype(BF16)

    @pl.when(core == 0)
    def _():
        pl.semaphore_wait(far_sem, 1)

    second = []
    for s in range(1, Z):
        second.append(exchange(sums.at[(z + s) // Z], got2.at[s - 1], X - 2 + s, z_peers[s - 1]))
        second[-1].start()

    @pl.when(ahead)
    def _():
        forward(0)
        lax.fori_loop(EARLY_AHEAD * STEPS, SUBS, causal, 0)
        forward(1)

    @pl.when(~ahead)
    def _():
        lax.fori_loop(BESIDE_FIRST, SUBS, causal, 0)
        forward(0)

    for moved in second:
        moved.wait_recv()
    along_z = got2[0].astype(F32)
    for s in range(1, Z - 1):
        along_z = along_z + got2[s].astype(F32)
    for to in range(X):
        part = along_z
        for s in range(X):
            if s < to:
                part = part + got1[s][:, :HD]
            elif s > to:
                part = part + got1[s][:, HD:]
        give3[to] = part
    got3[x] = give3[x]

    third = []
    for s in range(1, X):
        third.append(exchange(give3.at[(x + s) % X], got3.at[x], X + Z - 3 + s, x_peers[s - 1]))
        third[-1].start()

    @pl.when(ahead)
    def _():
        forward(LOCALS)
        forward(LOCALS + 1)

    @pl.when(~ahead)
    def _():
        forward(LOCALS)

    for moved in third:
        moved.wait_recv()
    read_state[...] = split_two(got3[...].reshape(HD, HD))

    gain_load.wait()
    gain = gain_ref[...]

    def give_state():
        gathered[head, STATE_AT:GAIN_AT, :] = read_state[:, :HD]
        gain_high = gain.astype(BF16).astype(F32)
        gain_row = lax.broadcasted_iota(jnp.int32, (16, HD), 0)
        gathered[head, GAIN_AT:GATHERED, :] = jnp.where(
            gain_row == 0, gain_high, jnp.where(gain_row == 1, gain - gain_high, 0.0)
        ).astype(BF16)
        give(STATE)

    def norm(unit):
        rows = slice(unit * UNIT, (unit + 1) * UNIT)
        attended = dot_two(q[rows, :], read_state[...]) + local[rows, :]
        gathered[head, rows, :] = normalize(attended, gain)
        give(unit)

    def project(unit):
        def one(step, _):
            rows = pl.ds(pl.multiple_of(step * SUB, SUB), SUB)
            normed = jnp.concatenate([gathered[h, rows, :] for h in range(HEADS)], axis=1)
            out[rows, :] = jnp.dot(normed, w[...], preferred_element_type=F32).astype(BF16)
            return 0

        lax.fori_loop(unit * STEPS, (unit + 1) * STEPS, one, 0)

    def early(step, _):
        rows = pl.ds(pl.multiple_of(step * SUB, SUB), SUB)
        local_rows = pl.ds(pl.multiple_of(ROWS + step * SUB, SUB), SUB)
        normed = []
        for h in range(HEADS):
            gains = gathered[h, GAIN_AT:GATHERED, :].astype(F32)
            attended = jnp.dot(
                gathered[h, rows, :], gathered[h, STATE_AT:GAIN_AT, :], preferred_element_type=F32
            ) + gathered[h, local_rows, :].astype(F32)
            normed.append(normalize(attended, gains[0:1] + gains[1:2]))
        out[rows, :] = jnp.dot(
            jnp.concatenate(normed, axis=1), w[...], preferred_element_type=F32
        ).astype(BF16)
        return 0

    w_load.wait()

    def drain(part, which=range(9)):
        for slot in slots(part):
            if slot in which:
                copy(part, slot).wait_send()

    def finish(early_units, given):
        units = list(range(early_units, UNITS))
        before = [part for unit in range(early_units) for part in (unit, LOCALS + unit)]
        give_state()
        for unit in units[:given]:
            norm(unit)
        for part in before:
            pass_far(part)
        forward(STATE)
        pass_far(STATE)
        sent = before + [STATE]
        for i, unit in enumerate(units):
            if i + given < len(units):
                norm(units[i + given])
            forward(unit)
            if i < early_units:
                arrived(i, LOCALS + i, *([STATE] if i == 0 else []))
                lax.fori_loop(i * STEPS, (i + 1) * STEPS, early, 0)
            if i > 1:
                pass_far(units[i - 2])
            if i > 2:
                arrived(units[i - 3])
                project(units[i - 3])
            if i > 0:
                for part in sent[:2]:
                    drain(part)
                sent = sent[2:]
            else:
                for moved in first + second + third:
                    moved.wait_send()
        pass_far(units[-2])
        for part in sent + units[:-2]:
            drain(part)
        arrived(units[-3])
        project(units[-3])
        arrived(units[-2])
        project(units[-2])
        pass_far(units[-1])
        drain(units[-2])
        drain(units[-1], range(SIB_A))
        arrived(units[-1])
        project(units[-1])
        drain(units[-1], (SIB_A, SIB_B))

    @pl.when(ahead)
    def _():
        finish(EARLY_AHEAD, GIVEN_AHEAD)

    @pl.when(~ahead)
    def _():
        finish(EARLY_ELSE, GIVEN_ELSE)


def body(queries, keys, values, prefix, norm_gain, out_weight):
    def hbm(array):
        return pltpu.with_memory_space_constraint(array, pltpu.HBM)

    anywhere = pl.BlockSpec(memory_space=pl.ANY)
    exchanges = 2 * (X - 1) + Z - 1
    return pl.pallas_call(
        kernel,
        out_shape=pltpu.VMEM((ROWS, COLS), BF16),
        in_specs=[
            anywhere, anywhere, anywhere,
            pl.BlockSpec(memory_space=pltpu.SMEM),
            anywhere, anywhere,
        ],
        out_specs=pl.BlockSpec(memory_space=pltpu.VMEM),
        scratch_shapes=[
            pltpu.VMEM((ROWS, HD), BF16),
            pltpu.VMEM((ROWS, HD), BF16),
            pltpu.VMEM((ROWS, HD), BF16),
            pltpu.VMEM((HEADS * HD, COLS), BF16),
            pltpu.VMEM((1, HD), F32),
            pltpu.VMEM((ROWS, HD), F32),
            pltpu.VMEM((HEADS, GATHERED, HD), BF16),
            pltpu.VMEM((HD, 2 * HD), F32),
            pltpu.VMEM((SUBS, HD, 2 * HD), BF16),
            pltpu.VMEM((HD, 2 * HD), BF16),
            pltpu.VMEM((HD, 2 * HD), BF16),
            pltpu.VMEM((X, QUARTER, 2 * HD), F32),
            pltpu.VMEM((2, QUARTER, HD), BF16),
            pltpu.VMEM((Z - 1, QUARTER, HD), BF16),
            pltpu.VMEM((X, QUARTER, HD), F32),
            pltpu.VMEM((X, QUARTER, HD), F32),
            pltpu.SemaphoreType.REGULAR,
            pltpu.SemaphoreType.REGULAR,
            pltpu.SemaphoreType.DMA((8,)),
            pltpu.SemaphoreType.DMA((exchanges,)),
            pltpu.SemaphoreType.DMA((exchanges,)),
            pltpu.SemaphoreType.DMA((len(PARTS), 9)),
            pltpu.SemaphoreType.DMA((len(PARTS), 9)),
        ],
        compiler_params=pltpu.CompilerParams(
            collective_id=0, has_side_effects=True, vmem_limit_bytes=40 * 2**20
        ),
        cost_estimate=pl.CostEstimate(
            flops=2 * ROWS * (8 * HD * COLS + 1024 * HD), bytes_accessed=8 * 2**20, transcendentals=ROWS
        ),
    )(hbm(queries), hbm(keys), hbm(values), prefix, hbm(norm_gain.reshape(1, HD)), hbm(out_weight))


def solution(mesh):
    return jax.shard_map(
        body,
        mesh=mesh,
        in_specs=(
            P("ctx", "head"),
            P("ctx", "head"),
            P("ctx", "head"),
            P(),
            P("head"),
            P(None, "head"),
        ),
        out_specs=P("ctx", "head"),
        check_vma=False,
    )
```
